128 devices in a mesh: train: 8 (over y, x_hi), replica: 4 (over x_lo, core), ep: 4 (over z).
Axes of the slice: x: 4 (x_hi: 2, x_lo: 2; x = x_hi * 2 + x_lo), y: 4, z: 4, core: 2. Of those that a mesh axis runs over, the one named last changes fastest.
Arguments:
- master: float32 [8, 2048, 7168], P('ep', 'replica', 'train'), may hold values from -6 to 6
- gradient: bfloat16 [8, 2048, 7168], P('ep', 'replica', 'train'), may hold values from -1000 to 1000
- second: float32 [8, 2048, 7168], P('ep', 'replica', 'train'), may hold values from 0.1 to 2
- placement: int32 [4, 8], replicated, may hold values from 0 to 3, as said below
Outputs:
- master_new: float32 [8, 2048, 7168], P('ep', 'replica', 'train')
- second_new: float32 [8, 2048, 7168], P('ep', 'replica', 'train')
- quantized: bfloat16 [4, 4, 2, 2048, 7168], P('replica', 'ep', None, None, 'train')
- scales: float32 [4, 4, 2, 16, 56], P('replica', 'ep', None, None, 'train')
The draws below stay inside these ranges and needn't reach their ends.
Inputs may be any that keep to these rules, and one draw needn't show every extreme that they name: `placement`: in each row every ep index is named by exactly 2 experts.
All inputs are finite; a program needn't handle non-finite values. Where the reference program divides by a largest or mean magnitude, that divisor is 1e-20 or more.
Results may differ from the reference program's by a relative error of at most 0.006.
Values may be sent and summed in bfloat16 or wider, within the bound.
No kernel may reach another device: no remote copies, remote signals or barrier semaphores. Data moves between devices by JAX's collectives and lax.ppermute only.
A program may use at most 192 MiB of HBM per device.

```python
import math
import jax
import jax.numpy as jnp
from jax import lax

D = 7168
FF = 2048
EXP_DEV = 2
BLOCK = 128
EXPERTS = 8
N_REPLICA = 4
N_EP = 4


def draw_gradient(key, part):
    key = jax.random.fold_in(key, 11)
    first_key, second_key, third_key = jax.random.split(key, 3)
    base = jnp.clip(jax.random.normal(first_key, (EXPERTS, FF, D), jnp.float32), -6.0, 6.0)
    power = 0.5
    along_experts = jnp.arange(EXPERTS, dtype=jnp.float32)[:, None, None] / EXPERTS
    along_rows = jnp.arange(FF, dtype=jnp.float32)[None, :, None] / FF
    along_columns = jnp.arange(D, dtype=jnp.float32)[None, None, :] / D
    trend = jnp.exp(power * math.log(3.0) * (along_experts + along_rows + along_columns))
    row_scale = jnp.exp(jax.random.uniform(second_key, (EXPERTS, FF, 1), jnp.float32, 0.0, math.log(3.2)))
    column_scale = jnp.exp(jax.random.uniform(third_key, (EXPERTS, 1, D), jnp.float32, 0.0, math.log(3.2)))
    return (2.0 * base * trend * row_scale * column_scale).astype(jnp.bfloat16)


def draw_placement(key, part):
    key = jax.random.fold_in(key, 23)
    replica_keys = jax.random.split(key, N_REPLICA)
    orders = jax.vmap(lambda single: jax.random.permutation(single, EXPERTS))(replica_keys)
    return (orders // EXP_DEV).astype(jnp.int32)


def block_scale(own_key, shape, cuts, least, high):
    factor_of, own = 1.0, jax.random.fold_in(own_key, 6)
    for dim, parts in cuts:
        draws = jnp.exp(jax.random.uniform(jax.random.fold_in(own, dim), (parts,), jnp.float32, least / len(cuts), high / len(cuts)))
        factor_of = factor_of * jnp.repeat(draws, shape[dim] // parts).reshape([-1 if axis == dim else 1 for axis in range(len(shape))])
    return factor_of


def centred(rng, extent, spread, bound, cuts=(), kind=jnp.bfloat16):
    loudness = block_scale(rng, extent, cuts, -0.22, 0.18) if cuts else 1.0
    entries = jax.random.normal(rng, extent, jnp.float32) * spread * loudness
    return jnp.minimum(jnp.maximum(entries, -bound), bound).astype(kind)


def setup_inputs(seed: int = 0) -> dict:
    key_list = jax.random.split(jax.random.key(seed), 5)
    return {
        "master": centred(key_list[0], (EXPERTS, FF, D), 1.0, 6.0, ((0, 4), (1, 4), (2, 8)), jnp.float32),
        "gradient": draw_gradient(jax.random.fold_in(key_list[4], 71), 0),
        "second": jnp.clip(jnp.exp(math.log(2.0) - 2.9957323 * jax.random.uniform(key_list[2], (EXPERTS, FF, D), jnp.float32) ** block_scale(key_list[2], (EXPERTS, FF, D), ((0, 4), (1, 4), (2, 8)), -0.2, 0.2)), 0.1, 2.0),
        "placement": draw_placement(jax.random.fold_in(key_list[4], 71), 0),
    }


decay_rate = 0.95
step_size = 0.3

def block_quantize(values):
    full_shape = values.shape
    blocks = values.astype(jnp.float32).reshape(full_shape[:-2] + (full_shape[-2] // BLOCK, BLOCK, full_shape[-1] // BLOCK, BLOCK))
    largest = lax.optimization_barrier(jnp.max(jnp.abs(blocks), axis=(-3, -1))) + 1e-06
    scaled = (blocks / largest[..., :, None, :, None]).astype(jnp.bfloat16).reshape(full_shape)
    return (scaled, largest)

def slot_table(placement, holders, per_device):
    matches = (placement[:, None, :] == jnp.arange(holders, dtype=jnp.int32)[None, :, None]).astype(jnp.int32)
    rank_within = jnp.cumsum(matches, axis=-1) - 1
    expert_ids = jnp.arange(placement.shape[-1], dtype=jnp.int32)
    slot_numbers = jnp.arange(per_device, dtype=jnp.int32)
    selected = matches[..., None, :] * (rank_within[..., None, :] == slot_numbers[:, None]).astype(jnp.int32)
    return lax.optimization_barrier(jnp.sum(selected * expert_ids, axis=-1)).astype(jnp.int32)

def reference(master, gradient, second, placement):
    values = gradient.astype(jnp.float32)
    square_sum = jnp.sum(values * values)
    root_mean = jnp.sqrt(square_sum / (EXPERTS * FF * D) + 1e-06)
    clipped = values / root_mean
    second_new = decay_rate * second + (1.0 - decay_rate) * clipped * clipped
    master_new = master - step_size * clipped / (jnp.sqrt(second_new) + 1e-08)
    weights = master_new.astype(jnp.bfloat16)
    scaled, largest = block_quantize(weights)
    slot_experts = slot_table(placement, N_EP, EXP_DEV)
    return (master_new, second_new, scaled[slot_experts], largest[slot_experts])
```

```python
import functools

import jax
import jax.numpy as jnp
from jax import lax
from jax.experimental import pallas as pl
from jax.experimental.pallas import tpu as pltpu
from jax.sharding import PartitionSpec as P

BLOCK = 128
decay_rate = 0.95
step_size = 0.3

ANY = pl.BlockSpec(memory_space=pl.ANY)
SMEM = pl.BlockSpec(memory_space=pltpu.SMEM)
VMEM = pl.BlockSpec(memory_space=pltpu.VMEM)
HBM = pl.BlockSpec(memory_space=pltpu.HBM)
LIMIT = pltpu.CompilerParams(vmem_limit_bytes=8 << 20)


def held(value):
    return pltpu.with_memory_space_constraint(value, pltpu.VMEM)


def cost(bytes_accessed, flops=0):
    return pl.CostEstimate(flops=flops, bytes_accessed=bytes_accessed, transcendentals=0)


def squares_kernel(gradient_ref, out_ref):
    experts, rows, cols = gradient_ref.shape
    step = 64
    total = jnp.zeros((8, cols), jnp.float32)
    for expert in range(experts):

        def add(i, total):
            values = gradient_ref[expert, pl.ds(pl.multiple_of(i * step, step), step), :].astype(jnp.float32)
            return total + jnp.sum((values * values).reshape(step // 8, 8, cols), axis=0)

        total = lax.fori_loop(0, rows // step, add, total)
    out_ref[...] = sum(total[:, c : c + 128] for c in range(0, cols, 128))


def local_squares(gradient):
    return pl.pallas_call(
        squares_kernel,
        in_specs=[VMEM],
        out_specs=VMEM,
        out_shape=jax.ShapeDtypeStruct((8, 128), jnp.float32),
        cost_estimate=cost(gradient.size * 2, gradient.size * 2),
        compiler_params=LIMIT,
        name="local_squares",
    )(held(gradient))


def all_sum(part):
    n_train, n_replica, n_ep = (lax.axis_size(a) for a in ("train", "replica", "ep"))

    def over(value, axes, orders):
        return value + sum(lax.ppermute(value, axes, order) for order in orders)

    part = over(part, "ep", [[(i, (i + k) % n_ep) for i in range(n_ep)] for k in range(1, n_ep)])
    part = over(
        part, "train", [[(i, (i + 2 * k) % n_train) for i in range(n_train)] for k in range(1, n_train // 2)]
    )
    pairs = [(t, r) for t in range(n_train) for r in range(n_replica)]
    flips = [(0, 2)] + ([(1, 0), (1, 2)] if n_train > 1 else [])
    part = over(
        part,
        ("train", "replica"),
        [[(t * n_replica + r, (t ^ ft) * n_replica + (r ^ fr)) for t, r in pairs] for ft, fr in flips],
    )
    return over(part, "replica", [[(r, r ^ 1) for r in range(n_replica)]])


def update_kernel(count, chunk, total_ref, master_ref, gradient_ref, second_ref, master_out, second_out, weights_out):
    square_sum = jnp.sum(total_ref[...], axis=(0, 1), keepdims=True)
    scale = 1.0 / jnp.sqrt(square_sum / count + 1e-06)
    step = 32
    for expert in range(master_ref.shape[0]):

        @pl.loop(0, BLOCK // step)
        def _(i):
            here = pl.ds(pl.multiple_of(i * step, step), step)
            rows = pl.ds(pl.multiple_of(chunk * BLOCK + i * step, step), step)
            clipped = gradient_ref[expert, rows, :].astype(jnp.float32) * scale
            second_new = decay_rate * second_ref[expert, rows, :] + (1.0 - decay_rate) * clipped * clipped
            master_new = master_ref[expert, rows, :] - step_size * clipped / (jnp.sqrt(second_new) + 1e-08)
            second_out[expert, here, :] = second_new
            master_out[expert, here, :] = master_new
            weights_out[expert, here, :] = master_new.astype(jnp.bfloat16)


def update_rows(count, total, master, gradient, second, chunk):
    experts, rows, cols = master.shape
    shape = (experts, BLOCK, cols)
    size = experts * BLOCK * cols
    return pl.pallas_call(
        functools.partial(update_kernel, count, chunk),
        in_specs=[VMEM] * 4,
        out_specs=[VMEM] * 3,
        out_shape=[pltpu.VMEM(shape, jnp.float32), pltpu.VMEM(shape, jnp.float32), pltpu.VMEM(shape, jnp.bfloat16)],
        cost_estimate=cost(size * 20, size * 20),
        compiler_params=LIMIT,
        name="update_rows",
    )(total, held(master), held(gradient), held(second))


def store_kernel(chunk, *refs):
    pieces, outs, sems = refs[:2], refs[-3:-1], refs[-1]
    copies = [
        pltpu.make_async_copy(
            piece.at[expert], out.at[expert, pl.ds(chunk * BLOCK, BLOCK), :], sems.at[number, expert]
        )
        for number, (piece, out) in enumerate(zip(pieces, outs))
        for expert in range(piece.shape[0])
    ]
    for copy in copies:
        copy.start()
    for copy in copies:
        copy.wait()


def store_rows(pieces, chunk, shape, earlier):
    return pl.pallas_call(
        functools.partial(store_kernel, chunk),
        in_specs=[VMEM] * 2 + [ANY] * len(earlier),
        out_specs=[HBM] * 2,
        out_shape=[jax.ShapeDtypeStruct(shape, jnp.float32)] * 2,
        input_output_aliases={2: 0, 3: 1} if earlier else {},
        scratch_shapes=[pltpu.SemaphoreType.DMA((2, shape[0]))],
        cost_estimate=cost(2 * pieces[0].size * 4),
        compiler_params=LIMIT,
        name="store_rows",
    )(*(held(p) for p in pieces), *earlier)


def slot_table(placement, holders, per_device):
    matches = (placement[:, None, :] == jnp.arange(holders, dtype=jnp.int32)[None, :, None]).astype(jnp.int32)
    rank_within = jnp.cumsum(matches, axis=-1) - 1
    expert_ids = jnp.arange(placement.shape[-1], dtype=jnp.int32)
    slot_numbers = jnp.arange(per_device, dtype=jnp.int32)
    selected = matches[..., None, :] * (rank_within[..., None, :] == slot_numbers[:, None]).astype(jnp.int32)
    return jnp.sum(selected * expert_ids, axis=-1)


def pick_kernel(copies, n, table_ref, *refs):
    arrays, outs = refs[:n], refs[n:]
    for entry, first, out, place in copies:
        code = table_ref[entry]
        for steps in range(4):

            @pl.when(code // 2 == steps)
            def _():
                outs[out][place] = arrays[first + steps][code % 2]


def pick(table, arrays, copies, out_sizes):
    rows, cols = arrays[0].shape[1:]
    return pl.pallas_call(
        functools.partial(pick_kernel, copies, len(arrays)),
        in_specs=[SMEM] + [VMEM] * len(arrays),
        out_specs=[VMEM] * len(out_sizes),
        out_shape=[pltpu.VMEM((n, rows, cols), jnp.bfloat16) for n in out_sizes],
        cost_estimate=cost(len(copies) * rows * cols * 4),
        compiler_params=LIMIT,
        name="pick_slots",
    )(table, *(held(a) for a in arrays))


def quantize_kernel(chunk, places, replica_ref, *refs):
    n = len({place[0] for place in places})
    parts, earlier, (out_ref, scales_ref, ready, sems) = refs[:n], refs[n:-4], refs[-4:]
    scales_ref[...] = earlier[1][...] if earlier else jnp.zeros_like(scales_ref)
    rows, cols = parts[0].shape[1:]
    blocks = cols // BLOCK
    copies = []
    for number, (part, index, flip, slot) in enumerate(places):
        block_row = jnp.bitwise_xor(replica_ref[0], flip) * 4 + chunk
        tops = []
        for block in range(blocks):
            values = jnp.abs(parts[part][index, :, block * BLOCK : (block + 1) * BLOCK].astype(jnp.float32))
            tops.append(jnp.max(values.reshape(rows // 8, 8, BLOCK), axis=0).max(axis=0, keepdims=True))
        tops = jnp.concatenate(tops + [jnp.zeros((8 - blocks, BLOCK), jnp.float32)], axis=0)
        largest = jnp.max(tops, axis=1, keepdims=True) + 1e-06
        inverse = 1.0 / largest
        for block in range(blocks):
            at = slice(block * BLOCK, (block + 1) * BLOCK)
            values = parts[part][index, :, at].astype(jnp.float32)
            ready[number, :, at] = (values * inverse[block : block + 1, :]).astype(jnp.bfloat16)
        lane = lax.broadcasted_iota(jnp.int32, (1, blocks), 1)
        line = jnp.zeros((1, blocks), jnp.float32)
        for block in range(blocks):
            line = jnp.where(lane == block, largest[block : block + 1, :], line)
        scales_ref[0, 0, slot, pl.ds(block_row, 1), :] = line
        target = out_ref.at[0, 0, slot, pl.ds(pl.multiple_of(block_row * BLOCK, BLOCK), BLOCK), :]
        copies.append(pltpu.make_async_copy(ready.at[number], target, sems.at[number]))
        copies[-1].start()
    for copy in copies:
        copy.wait()


def quantize(replica, parts, chunk, places, shape, earlier):
    rows, cols = parts[0].shape[1:]
    scales_shape = (1, 1, shape[2], shape[3] // BLOCK, cols // BLOCK)
    n = len(parts)
    return pl.pallas_call(
        functools.partial(quantize_kernel, chunk, places),
        in_specs=[SMEM] + [VMEM] * n + ([ANY, VMEM] if earlier else []),
        out_specs=[HBM, VMEM],
        out_shape=[jax.ShapeDtypeStruct(shape, jnp.bfloat16), jax.ShapeDtypeStruct(scales_shape, jnp.float32)],
        input_output_aliases={1 + n: 0} if earlier else {},
        scratch_shapes=[
            pltpu.VMEM((len(places), rows, cols), jnp.bfloat16),
            pltpu.SemaphoreType.DMA((len(places),)),
        ],
        cost_estimate=cost(8 * rows * cols * 4, 8 * rows * cols * 5),
        compiler_params=LIMIT,
        name="quantize_rows",
    )(replica, *(held(p) for p in parts), *earlier)


def body(master, gradient, second, placement):
    n_train, n_replica, n_ep = (lax.axis_size(a) for a in ("train", "replica", "ep"))
    experts, rows, cols = master.shape
    chunks = rows // BLOCK
    count = float(master.size * n_train * n_replica * n_ep)
    replica, holder = lax.axis_index("replica"), lax.axis_index("ep")

    slots = slot_table(placement, n_ep, experts)[:, holder]
    order = jnp.bitwise_xor(replica, jnp.arange(n_replica, dtype=jnp.int32))
    named = slots[order].reshape(-1)
    table = 2 * ((named // 2 - holder) % n_ep) + named % 2
    replica_ref = replica[None]

    total = all_sum(local_squares(gradient))

    def up(value):
        return lax.ppermute(value, "ep", [(i, (i + 1) % n_ep) for i in range(n_ep)])

    def down(value):
        return lax.ppermute(value, "ep", [(i, (i - 1) % n_ep) for i in range(n_ep)])

    def flip(value, by):
        return lax.ppermute(value, "replica", [(i, i ^ by) for i in range(n_replica)])

    updated = [update_rows(count, total, master, gradient, second, chunk) for chunk in range(chunks)]
    weights = [u[2] for u in updated]

    def gather(piece, forward_up):
        before, after = up(piece), down(piece)
        return [piece, after, up(before) if forward_up else down(after), before]

    shape = (1, 1, experts, n_replica * rows, cols)
    crossed = flip(weights[0], 2)
    parts = {}
    for chunk in range(1, chunks):
        arrays = gather(weights[chunk], chunk % 2 == 1)
        copies = [(2 * j + k, 0, j, k) for j in (2, 3, 1, 0) for k in range(2)]
        picked = pick(table, arrays, copies, [2] * 4)
        parts[chunk] = [picked[0]] + [flip(picked[j], j) for j in (1, 2, 3)]
    arrays = gather(weights[0], False) + gather(crossed, True)
    copies = [(2 * j + k, 4 * g, j, 2 * g + k) for j in (1, 0) for g in range(2) for k in range(2)]
    mine, other = pick(table, arrays, copies, [4, 4])
    parts[0] = [mine, flip(other, 1)]

    result = ()
    for chunk in range(1, chunks):
        places = [(j, k, j, k) for j in range(4) for k in range(2)]
        result = quantize(replica_ref, parts[chunk], chunk, places, shape, tuple(result))
    places = [(j, 2 * g + k, j ^ (2 * g), k) for j in range(2) for g in range(2) for k in range(2)]
    result = quantize(replica_ref, parts[0], 0, places, shape, tuple(result))
    new = ()
    for chunk in range(chunks):
        new = store_rows(updated[chunk][:2], chunk, master.shape, tuple(new))
    return (*new, *result)


def solution(mesh):
    return jax.shard_map(
        body,
        mesh=mesh,
        in_specs=(
            P("ep", "replica", "train"),
            P("ep", "replica", "train"),
            P("ep", "replica", "train"),
            P(),
        ),
        out_specs=(
            P("ep", "replica", "train"),
            P("ep", "replica", "train"),
            P("replica", "ep", None, None, "train"),
            P("replica", "ep", None, None, "train"),
        ),
        check_vma=False,
    )
```

```python
import functools

import jax
import jax.numpy as jnp
from jax import lax
from jax.experimental import pallas as pl
from jax.experimental.pallas import tpu as pltpu
from jax.sharding import PartitionSpec as P

BLOCK = 128
decay_rate = 0.95
step_size = 0.3

ANY = pl.BlockSpec(memory_space=pl.ANY)
SMEM = pl.BlockSpec(memory_space=pltpu.SMEM)
VMEM = pl.BlockSpec(memory_space=pltpu.VMEM)
HBM = pl.BlockSpec(memory_space=pltpu.HBM)
LIMIT = pltpu.CompilerParams(vmem_limit_bytes=8 << 20)


def held(value):
    return pltpu.with_memory_space_constraint(value, pltpu.VMEM)


def outside(value):
    return pltpu.with_memory_space_constraint(value, pltpu.HBM)


def kept(shape, dtype):
    return pltpu.VMEM(shape, dtype)


def cost(bytes_accessed, flops=0):
    return pl.CostEstimate(flops=flops, bytes_accessed=bytes_accessed, transcendentals=0)


def squares_kernel(gradient_ref, out_ref):
    experts, rows, cols = gradient_ref.shape
    step = 32
    total = jnp.zeros((8, cols), jnp.float32)
    for expert in range(experts):

        def add(i, total):
            values = gradient_ref[expert, pl.ds(pl.multiple_of(i * step, step), step), :].astype(jnp.float32)
            return total + jnp.sum((values * values).reshape(step // 8, 8, cols), axis=0)

        total = lax.fori_loop(0, rows // step, add, total)
    tile = sum(total[:, c : c + 128] for c in range(0, cols, 128))
    out_ref[...] = jnp.broadcast_to(jnp.sum(tile, axis=0, keepdims=True), out_ref.shape)


def local_squares(gradient, devices):
    return pl.pallas_call(
        squares_kernel,
        in_specs=[VMEM],
        out_specs=VMEM,
        out_shape=jax.ShapeDtypeStruct((devices, 128), jnp.float32),
        cost_estimate=cost(gradient.size * 2, gradient.size * 2),
        compiler_params=LIMIT,
        name="local_squares",
    )(held(gradient))


def load_kernel(chunk, n, *refs):
    sources, outs, sems = refs[:n], refs[-n - 1 : -1], refs[-1]
    copies = [
        pltpu.make_async_copy(
            source.at[expert, pl.ds(chunk * BLOCK, BLOCK), :], out.at[expert], sems.at[number, expert]
        )
        for number, (source, out) in enumerate(zip(sources, outs))
        for expert in range(out.shape[0])
    ]
    for copy in copies:
        copy.start()
    for copy in copies:
        copy.wait()


def load_rows(values, chunk, after):
    n = len(values)
    shapes = [(value.shape[0], BLOCK, value.shape[2]) for value in values]
    return pl.pallas_call(
        functools.partial(load_kernel, chunk, n),
        in_specs=[HBM] * n + [ANY] * len(after),
        out_specs=[VMEM] * n,
        out_shape=[kept(shape, value.dtype) for shape, value in zip(shapes, values)],
        scratch_shapes=[pltpu.SemaphoreType.DMA((n, shapes[0][0]))],
        cost_estimate=cost(sum(2 * a * b * c * 4 for a, b, c in shapes)),
        compiler_params=LIMIT,
        name="load_rows",
    )(*(outside(value) for value in values), *after)


def new_rows(scale, master, gradient, second):
    clipped = gradient.astype(jnp.float32) * scale
    second_new = decay_rate * second + (1.0 - decay_rate) * clipped * clipped
    return master - step_size * clipped / (jnp.sqrt(second_new) + 1e-08), second_new


def scale_of(count, total_ref):
    square_sum = jnp.sum(jnp.sum(total_ref[...], axis=0, keepdims=True), axis=1, keepdims=True)
    return 1.0 / jnp.sqrt(square_sum / count + 1e-06)


def weights_kernel(count, total_ref, master_ref, gradient_ref, second_ref, weights_out):
    scale = scale_of(count, total_ref)
    step = 32
    for expert in range(master_ref.shape[0]):

        @pl.loop(0, BLOCK // step)
        def _(i):
            here = pl.ds(pl.multiple_of(i * step, step), step)
            master_new, _ = new_rows(
                scale, master_ref[expert, here, :], gradient_ref[expert, here, :], second_ref[expert, here, :]
            )
            weights_out[expert, here, :] = master_new.astype(jnp.bfloat16)


def first_weights(count, total, master, gradient, second):
    return pl.pallas_call(
        functools.partial(weights_kernel, count),
        in_specs=[VMEM] * 4,
        out_specs=VMEM,
        out_shape=kept(master.shape, jnp.bfloat16),
        cost_estimate=cost(master.size * 12, master.size * 20),
        compiler_params=LIMIT,
        name="first_weights",
    )(held(total), held(master), held(gradient), held(second))


def update_kernel(count, chunk, total_ref, *refs):
    sources, (master_out, second_out, weights_out, *scratch) = refs[:3], refs[-10:]
    master_in, gradient_in, second_in, master_new, second_new, in_sems, out_sems = scratch
    scale = scale_of(count, total_ref)
    experts = weights_out.shape[0]
    step, half = 32, BLOCK // 2
    pieces = [(expert, part) for expert in range(experts) for part in range(2)]

    def rows_of(part):
        return pl.ds(part * half, half), pl.ds(chunk * BLOCK + part * half, half)

    arriving, leaving = {}, []
    for expert, part in pieces:
        here, there = rows_of(part)
        arriving[expert, part] = [
            pltpu.make_async_copy(source.at[expert, there, :], place.at[expert, here, :], in_sems.at[n, expert, part])
            for n, (source, place) in enumerate(zip(sources, (master_in, gradient_in, second_in)))
        ]
        for copy in arriving[expert, part]:
            copy.start()
    for expert, part in pieces:
        for copy in arriving[expert, part]:
            copy.wait()

        @pl.loop(0, half // step)
        def _(i):
            here = pl.ds(pl.multiple_of(part * half + i * step, step), step)
            master, second = new_rows(
                scale, master_in[expert, here, :], gradient_in[expert, here, :], second_in[expert, here, :]
            )
            master_new[expert, here, :] = master
            second_new[expert, here, :] = second
            weights_out[expert, here, :] = master.astype(jnp.bfloat16)

        here, there = rows_of(part)
        for n, (place, out) in enumerate(((master_new, master_out), (second_new, second_out))):
            copy = pltpu.make_async_copy(
                place.at[expert, here, :], out.at[expert, there, :], out_sems.at[n, expert, part]
            )
            copy.start()
            leaving.append(copy)
    for copy in leaving:
        copy.wait()


def update_rows(count, total, master, gradient, second, chunk, earlier, after):
    experts, rows, cols = master.shape
    shape = (experts, BLOCK, cols)
    size = experts * BLOCK * cols
    return pl.pallas_call(
        functools.partial(update_kernel, count, chunk),
        in_specs=[VMEM] + [HBM] * 3 + [ANY] * (len(earlier) + len(after)),
        out_specs=[HBM, HBM, VMEM],
        out_shape=[
            jax.ShapeDtypeStruct(master.shape, jnp.float32),
            jax.ShapeDtypeStruct(master.shape, jnp.float32),
            kept(shape, jnp.bfloat16),
        ],
        input_output_aliases={4: 0, 5: 1} if earlier else {},
        scratch_shapes=[
            pltpu.VMEM(shape, jnp.float32),
            pltpu.VMEM(shape, jnp.bfloat16),
            pltpu.VMEM(shape, jnp.float32),
            pltpu.VMEM(shape, jnp.float32),
            pltpu.VMEM(shape, jnp.float32),
            pltpu.SemaphoreType.DMA((3, experts, 2)),
            pltpu.SemaphoreType.DMA((2, experts, 2)),
        ],
        cost_estimate=cost(size * 20, size * 20),
        compiler_params=LIMIT,
        name="update_rows",
    )(held(total), outside(master), outside(gradient), outside(second), *earlier, *after)


def slot_table(placement, holders, per_device):
    matches = (placement[:, None, :] == jnp.arange(holders, dtype=jnp.int32)[None, :, None]).astype(jnp.int32)
    rank_within = jnp.cumsum(matches, axis=-1) - 1
    expert_ids = jnp.arange(placement.shape[-1], dtype=jnp.int32)
    slot_numbers = jnp.arange(per_device, dtype=jnp.int32)
    selected = matches[..., None, :] * (rank_within[..., None, :] == slot_numbers[:, None]).astype(jnp.int32)
    return jnp.sum(selected * expert_ids, axis=-1)


def step_kernel(moves, n, table_ref, *refs):
    arrays, outs = refs[:n], refs[len(refs) - 1 - max(m[0] for m in moves) :]
    for out, place, entry, sources in moves:
        if entry is None:
            array, index = sources
            outs[out][place] = arrays[array][index]
            continue
        code = table_ref[entry]
        for steps, (low, high) in enumerate(sources):
            if low[0] == high[0]:

                @pl.when(code // 2 == steps)
                def _():
                    outs[out][place] = arrays[low[0]][low[1] + code % 2]

            else:
                for number, (array, index) in enumerate((low, high)):

                    @pl.when(code == 2 * steps + number)
                    def _():
                        outs[out][place] = arrays[array][index]


def make_step(table, outs, after=(), work=0):
    arrays, moves = [], []

    def number_of(array):
        for number, known in enumerate(arrays):
            if known is array:
                return number
        arrays.append(array)
        return len(arrays) - 1

    for out, pieces in enumerate(outs):
        for place, (first, second) in enumerate(pieces):
            if isinstance(first, int):
                sources = [tuple((number_of(a), i) for a, i in pair) for pair in second]
                moves.append((out, place, first, sources))
            else:
                moves.append((out, place, None, (number_of(first), second)))
    rows, cols = arrays[0].shape[1:]
    return pl.pallas_call(
        functools.partial(step_kernel, moves, len(arrays)),
        in_specs=[SMEM] + [VMEM] * len(arrays) + [ANY] * len(after),
        out_specs=[VMEM] * len(outs),
        out_shape=[kept((len(pieces), rows, cols), jnp.bfloat16) for pieces in outs],
        cost_estimate=cost(max(int(work * 3.3e6), len(moves) * rows * cols * 4)),
        compiler_params=LIMIT,
        name="make_step",
    )(table, *(held(a) for a in arrays), *after)


def quantize_kernel(places, replica_ref, *refs):
    n = len({place[0] for place in places})
    parts, earlier, (out_ref, scales_ref, ready, sems) = refs[:n], refs[n:-4], refs[-4:]
    scales_ref[...] = earlier[1][...] if earlier else jnp.zeros_like(scales_ref)
    rows, cols = parts[0].shape[1:]
    blocks = cols // BLOCK
    copies = []
    for number, (part, index, flip, slot, chunk) in enumerate(places):
        block_row = jnp.bitwise_xor(replica_ref[0], flip) * 4 + chunk
        tops = []
        for block in range(blocks):
            values = jnp.abs(parts[part][index, :, block * BLOCK : (block + 1) * BLOCK].astype(jnp.float32))
            tops.append(jnp.max(values.reshape(rows // 8, 8, BLOCK), axis=0).max(axis=0, keepdims=True))
        tops = jnp.concatenate(tops + [jnp.zeros((8 - blocks, BLOCK), jnp.float32)], axis=0)
        largest = jnp.max(tops, axis=1, keepdims=True) + 1e-06
        inverse = 1.0 / largest
        for block in range(blocks):
            at = slice(block * BLOCK, (block + 1) * BLOCK)
            values = parts[part][index, :, at].astype(jnp.float32)
            ready[number, :, at] = (values * inverse[block : block + 1, :]).astype(jnp.bfloat16)
        lane = lax.broadcasted_iota(jnp.int32, (1, blocks), 1)
        line = jnp.zeros((1, blocks), jnp.float32)
        for block in range(blocks):
            line = jnp.where(lane == block, largest[block : block + 1, :], line)
        scales_ref[0, 0, slot, pl.ds(block_row, 1), :] = line
        target = out_ref.at[0, 0, slot, pl.ds(pl.multiple_of(block_row * BLOCK, BLOCK), BLOCK), :]
        copies.append(pltpu.make_async_copy(ready.at[number], target, sems.at[number]))
        copies[-1].start()
    for copy in copies:
        copy.wait()


def quantize(replica, parts, places, shape, earlier):
    rows, cols = parts[0].shape[1:]
    scales_shape = (1, 1, shape[2], shape[3] // BLOCK, cols // BLOCK)
    n = len(parts)
    return pl.pallas_call(
        functools.partial(quantize_kernel, tuple(places)),
        in_specs=[SMEM] + [VMEM] * n + ([ANY, VMEM] if earlier else []),
        out_specs=[HBM, VMEM],
        out_shape=[jax.ShapeDtypeStruct(shape, jnp.bfloat16), jax.ShapeDtypeStruct(scales_shape, jnp.float32)],
        input_output_aliases={1 + n: 0} if earlier else {},
        scratch_shapes=[
            pltpu.VMEM((len(places), rows, cols), jnp.bfloat16),
            pltpu.SemaphoreType.DMA((len(places),)),
        ],
        cost_estimate=cost(len(places) * rows * cols * 4, len(places) * rows * cols * 5),
        compiler_params=pltpu.CompilerParams(vmem_limit_bytes=12 << 20),
        name="quantize_rows",
    )(replica, *(held(p) for p in parts), *earlier)


def body(master, gradient, second, placement):
    n_train, n_replica, n_ep = (lax.axis_size(a) for a in ("train", "replica", "ep"))
    experts, rows, cols = master.shape
    count = float(master.size * n_train * n_replica * n_ep)
    replica, holder = lax.axis_index("replica"), lax.axis_index("ep")

    slots = slot_table(placement, n_ep, experts)[:, holder]
    order = jnp.bitwise_xor(replica, jnp.arange(n_replica, dtype=jnp.int32))
    named = slots[order].reshape(-1)
    table = 2 * ((named // 2 - holder) % n_ep) + named % 2
    replica_ref = replica[None]

    devices = ("train", "replica", "ep")
    part = local_squares(gradient, n_train * n_replica * n_ep)
    master1, gradient1, second1 = load_rows((master, gradient, second), 1, (part,))
    total = lax.all_to_all(part, devices, 0, 0, tiled=True)

    def send(value, axis, order, name):
        with jax.named_scope(name):
            return lax.ppermute(value, axis, order)

    def up(value, name):
        return send(value, "ep", [(i, (i + 1) % n_ep) for i in range(n_ep)], name + "_up")

    def down(value, name):
        return send(value, "ep", [(i, (i - 1) % n_ep) for i in range(n_ep)], name + "_down")

    def flip(value, by, name):
        return send(value, "replica", [(i, i ^ by) for i in range(n_replica)], name)

    def step(name, outs, after=()):
        with jax.named_scope(name):
            return make_step(table, outs, tuple(after))

    def both(array, first=0):
        return [(array, first), (array, first + 1)]

    def slots_of(flips, here, above, far, below):
        return [(2 * j + k, [here, above, far, below]) for j in flips for k in range(2)]

    def update(chunk, earlier, after=()):
        *new, weights = update_rows(count, total, master, gradient, second, chunk, tuple(earlier), after)
        return new, weights

    def place(chunk, *entries):
        return [(part, index + k, j, k, chunk) for part, index, j in entries for k in range(2)]

    shape = (1, 1, experts, n_replica * rows, cols)

    w1 = first_weights(count, total, master1, gradient1, second1)
    below1, above1 = up(w1, "one"), down(w1, "one")
    new, e = update(0, (), (w1,))
    new, w2 = update(2, new)

    a, b = step("turn_one", [[(below1, 0)] + both(w2), [(above1, 1)] + both(w2)], (e,))
    below2, above2 = up(a, "two"), down(b, "two")
    f = flip(e, 2, "cross")
    new, w3 = update(3, new, (a,))

    def pick(name, ring, flips, after):
        outs = [sum((slots_of((j,), *ring) for j in group), []) for group in flips]
        return step("pick_" + name, outs + [slots_of((0,), *ring)], after)

    a, b = step("turn_two", [[(below2, 1)] + both(w3), [(above2, 2)] + both(w3)], (f,))
    below3, above3 = up(a, "three"), down(b, "three")
    ring1 = (both(w1), both(above1), [(below2, 0), (above2, 0)], both(below1))
    x, o1, s1 = pick("one", ring1, ((2, 3), (1,)), (a,))
    y1 = flip(x, 2, "chip_one")
    new, again = update(1, new, (s1,))

    a, b = step("turn_three", [[(below3, 1)] + both(e), [(above3, 2)] + both(e)], (s1, again))
    below4, above4 = up(a, "four"), down(b, "four")
    z1 = flip(o1, 1, "core_one")
    ring2 = (both(w2), both(above2, 1), [(below3, 0), (above3, 0)], both(below2, 1))
    x, o2, s2 = pick("two", ring2, ((2, 3), (1,)), (a,))
    y2 = flip(x, 2, "chip_two")

    a, b = step("turn_four", [[(below4, 1)] + both(f), [(above4, 2)] + both(f)], (s2, y1, z1))
    below5, above5 = up(a, "five"), down(b, "five")
    ring3 = (both(w3), both(above3, 1), [(below4, 0), (above4, 0)], both(below3, 1))
    x3, v3, o3, s3 = pick("three", ring3, ((2,), (3,), (1,)), (a,))
    x3 = flip(x3, 2, "chip_three")
    z2 = flip(o2, 1, "core_two")
    (c,) = step("pass_one", [both(y1, 2)], (s3,))
    t1 = flip(c, 1, "core_pass")

    a, b = step("turn_five", [[(below5, 1)], [(above5, 2)]], (c, y2, x3, z2, t1))
    far_low_f, far_high_f = up(a, "last"), down(b, "last")
    v3 = flip(v3, 3, "both_three")
    places = place(1, (0, 0, 0), (1, 0, 1), (2, 0, 2), (3, 0, 3))
    result = quantize(replica_ref, [s1, z1, y1, t1], places, shape, ())

    ring_e = (both(e), both(above4, 1), [(below5, 0), (above5, 0)], both(below4, 1))
    ring_f = (both(f), both(above5, 1), [(far_low_f, 0), (far_high_f, 0)], both(below5, 1))
    c, sf, se = step(
        "join_last",
        [
            both(y2, 2) + both(o3) + slots_of((1,), *ring_e) + slots_of((1,), *ring_f),
            slots_of((0,), *ring_f),
            slots_of((0,), *ring_e),
        ],
        (result[1], v3),
    )
    z = flip(c, 1, "core_last")
    places = place(2, (0, 0, 0), (1, 0, 1), (2, 0, 2)) + place(3, (3, 0, 0), (4, 0, 2), (5, 0, 3))
    places += place(0, (6, 0, 0), (7, 0, 2))
    result = quantize(replica_ref, [s2, z2, y2, s3, x3, v3, se, sf], places, shape, tuple(result))
    places = place(2, (0, 0, 3)) + place(3, (0, 2, 1)) + place(0, (0, 4, 1), (0, 6, 3))
    result = quantize(replica_ref, [z], places, shape, tuple(result))
    return (*new, *result)


def solution(mesh):
    return jax.shard_map(
        body,
        mesh=mesh,
        in_specs=(
            P("ep", "replica", "train"),
            P("ep", "replica", "train"),
            P("ep", "replica", "train"),
            P(),
        ),
        out_specs=(
            P("ep", "replica", "train"),
            P("ep", "replica", "train"),
            P("replica", "ep", None, None, "train"),
            P("replica", "ep", None, None, "train"),
        ),
        check_vma=False,
    )
```

```python
import functools

import jax
import jax.numpy as jnp
from jax import lax
from jax.experimental import pallas as pl
from jax.experimental.pallas import tpu as pltpu
from jax.sharding import PartitionSpec as P

BLOCK = 128
decay_rate = 0.95
step_size = 0.3

ANY = pl.BlockSpec(memory_space=pl.ANY)
SMEM = pl.BlockSpec(memory_space=pltpu.SMEM)
VMEM = pl.BlockSpec(memory_space=pltpu.VMEM)
HBM = pl.BlockSpec(memory_space=pltpu.HBM)
LIMIT = pltpu.CompilerParams(vmem_limit_bytes=8 << 20)


def held(value):
    return pltpu.with_memory_space_constraint(value, pltpu.VMEM)


def outside(value):
    return pltpu.with_memory_space_constraint(value, pltpu.HBM)


def kept(shape, dtype):
    return pltpu.VMEM(shape, dtype)


def cost(bytes_accessed, flops=0):
    return pl.CostEstimate(flops=flops, bytes_accessed=bytes_accessed, transcendentals=0)


def squares_kernel(gradient_ref, out_ref):
    experts, rows, cols = gradient_ref.shape
    step = 64
    total = jnp.zeros((8, cols), jnp.float32)
    for expert in range(experts):

        def add(i, total):
            values = gradient_ref[expert, pl.ds(pl.multiple_of(i * step, step), step), :].astype(jnp.float32)
            return total + jnp.sum((values * values).reshape(step // 8, 8, cols), axis=0)

        total = lax.fori_loop(0, rows // step, add, total)
    tile = sum(total[:, c : c + 128] for c in range(0, cols, 128))
    out_ref[...] = jnp.broadcast_to(jnp.sum(tile, axis=0, keepdims=True), out_ref.shape)


def local_squares(gradient, devices):
    return pl.pallas_call(
        squares_kernel,
        in_specs=[VMEM],
        out_specs=VMEM,
        out_shape=jax.ShapeDtypeStruct((devices, 128), jnp.float32),
        cost_estimate=cost(gradient.size * 2, gradient.size * 2),
        compiler_params=LIMIT,
        name="local_squares",
    )(held(gradient))


def load_kernel(chunk, n, *refs):
    sources, outs, sems = refs[:n], refs[-n - 1 : -1], refs[-1]
    copies = [
        pltpu.make_async_copy(
            source.at[expert, pl.ds(chunk * BLOCK, BLOCK), :], out.at[expert], sems.at[number, expert]
        )
        for number, (source, out) in enumerate(zip(sources, outs))
        for expert in range(out.shape[0])
    ]
    for copy in copies:
        copy.start()
    for copy in copies:
        copy.wait()


def load_rows(values, chunk, after):
    n = len(values)
    shapes = [(value.shape[0], BLOCK, value.shape[2]) for value in values]
    return pl.pallas_call(
        functools.partial(load_kernel, chunk, n),
        in_specs=[HBM] * n + [ANY] * len(after),
        out_specs=[VMEM] * n,
        out_shape=[kept(shape, value.dtype) for shape, value in zip(shapes, values)],
        scratch_shapes=[pltpu.SemaphoreType.DMA((n, shapes[0][0]))],
        cost_estimate=cost(sum(2 * a * b * c * 4 for a, b, c in shapes)),
        compiler_params=LIMIT,
        name="load_rows",
    )(*(outside(value) for value in values), *after)


def new_rows(scale, master, gradient, second):
    clipped = gradient.astype(jnp.float32) * scale
    second_new = decay_rate * second + (1.0 - decay_rate) * clipped * clipped
    return master - step_size * clipped / (jnp.sqrt(second_new) + 1e-08), second_new


def scale_of(count, total_ref):
    square_sum = jnp.sum(jnp.sum(total_ref[...], axis=0, keepdims=True), axis=1, keepdims=True)
    return 1.0 / jnp.sqrt(square_sum / count + 1e-06)


def weights_kernel(count, total_ref, master_ref, gradient_ref, second_ref, weights_out):
    scale = scale_of(count, total_ref)
    step = 32
    for expert in range(master_ref.shape[0]):

        @pl.loop(0, BLOCK // step)
        def _(i):
            here = pl.ds(pl.multiple_of(i * step, step), step)
            master_new, _ = new_rows(
                scale, master_ref[expert, here, :], gradient_ref[expert, here, :], second_ref[expert, here, :]
            )
            weights_out[expert, here, :] = master_new.astype(jnp.bfloat16)


def first_weights(count, total, master, gradient, second):
    return pl.pallas_call(
        functools.partial(weights_kernel, count),
        in_specs=[VMEM] * 4,
        out_specs=VMEM,
        out_shape=kept(master.shape, jnp.bfloat16),
        cost_estimate=cost(master.size * 12, master.size * 20),
        compiler_params=LIMIT,
        name="first_weights",
    )(held(total), held(master), held(gradient), held(second))


def update_kernel(count, chunk, total_ref, *refs):
    sources, (master_out, second_out, weights_out, *scratch) = refs[:3], refs[-10:]
    master_in, gradient_in, second_in, master_new, second_new, in_sems, out_sems = scratch
    scale = scale_of(count, total_ref)
    experts = weights_out.shape[0]
    step, half = 32, BLOCK // 2
    pieces = [(expert, part) for expert in range(experts) for part in range(2)]

    def rows_of(part):
        return pl.ds(part * half, half), pl.ds(chunk * BLOCK + part * half, half)

    arriving, leaving = {}, []
    for expert, part in pieces:
        here, there = rows_of(part)
        arriving[expert, part] = [
            pltpu.make_async_copy(source.at[expert, there, :], place.at[expert, here, :], in_sems.at[n, expert, part])
            for n, (source, place) in enumerate(zip(sources, (master_in, gradient_in, second_in)))
        ]
        for copy in arriving[expert, part]:
            copy.start()
    for expert, part in pieces:
        for copy in arriving[expert, part]:
            copy.wait()

        @pl.loop(0, half // step)
        def _(i):
            here = pl.ds(pl.multiple_of(part * half + i * step, step), step)
            master, second = new_rows(
                scale, master_in[expert, here, :], gradient_in[expert, here, :], second_in[expert, here, :]
            )
            master_new[expert, here, :] = master
            second_new[expert, here, :] = second
            weights_out[expert, here, :] = master.astype(jnp.bfloat16)

        here, there = rows_of(part)
        for n, (place, out) in enumerate(((master_new, master_out), (second_new, second_out))):
            copy = pltpu.make_async_copy(
                place.at[expert, here, :], out.at[expert, there, :], out_sems.at[n, expert, part]
            )
            copy.start()
            leaving.append(copy)
    for copy in leaving:
        copy.wait()


def update_rows(count, total, master, gradient, second, chunk, earlier, after):
    experts, rows, cols = master.shape
    shape = (experts, BLOCK, cols)
    size = experts * BLOCK * cols
    return pl.pallas_call(
        functools.partial(update_kernel, count, chunk),
        in_specs=[VMEM] + [HBM] * 3 + [ANY] * (len(earlier) + len(after)),
        out_specs=[HBM, HBM, VMEM],
        out_shape=[
            jax.ShapeDtypeStruct(master.shape, jnp.float32),
            jax.ShapeDtypeStruct(master.shape, jnp.float32),
            kept(shape, jnp.bfloat16),
        ],
        input_output_aliases={4: 0, 5: 1} if earlier else {},
        scratch_shapes=[
            pltpu.VMEM(shape, jnp.float32),
            pltpu.VMEM(shape, jnp.bfloat16),
            pltpu.VMEM(shape, jnp.float32),
            pltpu.VMEM(shape, jnp.float32),
            pltpu.VMEM(shape, jnp.float32),
            pltpu.SemaphoreType.DMA((3, experts, 2)),
            pltpu.SemaphoreType.DMA((2, experts, 2)),
        ],
        cost_estimate=cost(size * 20, size * 20),
        compiler_params=LIMIT,
        name="update_rows",
    )(held(total), outside(master), outside(gradient), outside(second), *earlier, *after)


def slot_table(placement, holders, per_device):
    matches = (placement[:, None, :] == jnp.arange(holders, dtype=jnp.int32)[None, :, None]).astype(jnp.int32)
    rank_within = jnp.cumsum(matches, axis=-1) - 1
    expert_ids = jnp.arange(placement.shape[-1], dtype=jnp.int32)
    slot_numbers = jnp.arange(per_device, dtype=jnp.int32)
    selected = matches[..., None, :] * (rank_within[..., None, :] == slot_numbers[:, None]).astype(jnp.int32)
    return jnp.sum(selected * expert_ids, axis=-1)


def step_kernel(moves, n, *refs):
    table_ref = refs[n]
    arrays, outs = refs[:n], refs[len(refs) - 1 - max(m[0] for m in moves) :]
    for out, place, entry, sources in moves:
        if entry is None:
            array, index = sources
            outs[out][place] = arrays[array][index]
            continue
        code = table_ref[entry]
        for steps, (low, high) in enumerate(sources):
            if low[0] == high[0]:

                @pl.when(code // 2 == steps)
                def _():
                    outs[out][place] = arrays[low[0]][low[1] + code % 2]

            else:
                for number, (array, index) in enumerate((low, high)):

                    @pl.when(code == 2 * steps + number)
                    def _():
                        outs[out][place] = arrays[array][index]


def make_step(table, outs, after=(), work=0):
    arrays, moves = [], []

    def number_of(array):
        for number, known in enumerate(arrays):
            if known is array:
                return number
        arrays.append(array)
        return len(arrays) - 1

    for out, pieces in enumerate(outs):
        for place, (first, second) in enumerate(pieces):
            if isinstance(first, int):
                sources = [tuple((number_of(a), i) for a, i in pair) for pair in second]
                moves.append((out, place, first, sources))
            else:
                moves.append((out, place, None, (number_of(first), second)))
    rows, cols = arrays[0].shape[1:]
    tables = [table] if any(move[2] is not None for move in moves) else []
    return pl.pallas_call(
        functools.partial(step_kernel, moves, len(arrays)),
        in_specs=[VMEM] * len(arrays) + [SMEM] * len(tables) + [ANY] * len(after),
        out_specs=[VMEM] * len(outs),
        out_shape=[kept((len(pieces), rows, cols), jnp.bfloat16) for pieces in outs],
        cost_estimate=cost(max(int(work * 3.3e6), len(moves) * rows * cols * 4)),
        compiler_params=LIMIT,
        name="make_step",
    )(*(held(a) for a in arrays), *tables, *after)


def quantize_kernel(places, *refs):
    n = len({place[0] for place in places})
    replica = lax.axis_index("replica")
    parts, earlier, (out_ref, scales_ref, ready, sems) = refs[:n], refs[n:-4], refs[-4:]
    scales_ref[...] = earlier[1][...] if earlier else jnp.zeros_like(scales_ref)
    rows, cols = parts[0].shape[1:]
    blocks = cols // BLOCK
    copies = []
    for number, (part, index, flip, slot, chunk) in enumerate(places):
        block_row = jnp.bitwise_xor(replica, flip) * 4 + chunk
        tops = []
        for block in range(blocks):
            values = jnp.abs(parts[part][index, :, block * BLOCK : (block + 1) * BLOCK].astype(jnp.float32))
            tops.append(jnp.max(values.reshape(rows // 8, 8, BLOCK), axis=0).max(axis=0, keepdims=True))
        tops = jnp.concatenate(tops + [jnp.zeros((8 - blocks, BLOCK), jnp.float32)], axis=0)
        largest = jnp.max(tops, axis=1, keepdims=True) + 1e-06
        inverse = 1.0 / largest
        for block in range(blocks):
            at = slice(block * BLOCK, (block + 1) * BLOCK)
            values = parts[part][index, :, at].astype(jnp.float32)
            ready[number, :, at] = (values * inverse[block : block + 1, :]).astype(jnp.bfloat16)
        lane = lax.broadcasted_iota(jnp.int32, (1, blocks), 1)
        line = jnp.zeros((1, blocks), jnp.float32)
        for block in range(blocks):
            line = jnp.where(lane == block, largest[block : block + 1, :], line)
        scales_ref[0, 0, slot, pl.ds(block_row, 1), :] = line
        target = out_ref.at[0, 0, slot, pl.ds(pl.multiple_of(block_row * BLOCK, BLOCK), BLOCK), :]
        copies.append(pltpu.make_async_copy(ready.at[number], target, sems.at[number]))
        copies[-1].start()
    for copy in copies:
        copy.wait()


def quantize(parts, places, shape, earlier):
    rows, cols = parts[0].shape[1:]
    scales_shape = (1, 1, shape[2], shape[3] // BLOCK, cols // BLOCK)
    n = len(parts)
    return pl.pallas_call(
        functools.partial(quantize_kernel, tuple(places)),
        in_specs=[VMEM] * n + ([ANY, VMEM] if earlier else []),
        out_specs=[HBM, VMEM],
        out_shape=[jax.ShapeDtypeStruct(shape, jnp.bfloat16), jax.ShapeDtypeStruct(scales_shape, jnp.float32)],
        input_output_aliases={n: 0} if earlier else {},
        scratch_shapes=[
            pltpu.VMEM((len(places), rows, cols), jnp.bfloat16),
            pltpu.SemaphoreType.DMA((len(places),)),
        ],
        cost_estimate=cost(len(places) * rows * cols * 4, len(places) * rows * cols * 5),
        compiler_params=pltpu.CompilerParams(vmem_limit_bytes=12 << 20),
        name="quantize_rows",
    )(*(held(p) for p in parts), *earlier)


def body(master, gradient, second, placement):
    n_train, n_replica, n_ep = (lax.axis_size(a) for a in ("train", "replica", "ep"))
    experts, rows, cols = master.shape
    count = float(master.size * n_train * n_replica * n_ep)
    replica, holder = lax.axis_index("replica"), lax.axis_index("ep")

    slots = slot_table(placement, n_ep, experts)[:, holder]
    order = jnp.bitwise_xor(replica, jnp.arange(n_replica, dtype=jnp.int32))
    named = slots[order].reshape(-1)
    table = 2 * ((named // 2 - holder) % n_ep) + named % 2

    devices = ("train", "replica", "ep")
    part = local_squares(gradient, n_train * n_replica * n_ep)
    master1, gradient1, second1 = load_rows((master, gradient, second), 1, (part, table))
    total = lax.all_to_all(part, devices, 0, 0, tiled=True)

    def send(value, axis, order, name):
        with jax.named_scope(name):
            return lax.ppermute(value, axis, order)

    def up(value, name):
        return send(value, "ep", [(i, (i + 1) % n_ep) for i in range(n_ep)], name + "_up")

    def down(value, name):
        return send(value, "ep", [(i, (i - 1) % n_ep) for i in range(n_ep)], name + "_down")

    def flip(value, by, name):
        return send(value, "replica", [(i, i ^ by) for i in range(n_replica)], name)

    def step(name, outs, after=()):
        with jax.named_scope(name):
            return make_step(table, outs, tuple(after))

    def both(array, first=0):
        return [(array, first), (array, first + 1)]

    def slots_of(flips, here, above, far, below):
        return [(2 * j + k, [here, above, far, below]) for j in flips for k in range(2)]

    def update(chunk, earlier, after=()):
        *new, weights = update_rows(count, total, master, gradient, second, chunk, tuple(earlier), after)
        return new, weights

    def place(chunk, *entries):
        return [(part, index + k, j, k, chunk) for part, index, j in entries for k in range(2)]

    shape = (1, 1, experts, n_replica * rows, cols)

    w1 = first_weights(count, total, master1, gradient1, second1)
    below1, above1 = up(w1, "one"), down(w1, "one")
    new, e = update(0, (), (w1,))
    new, w2 = update(2, new)

    (a,) = step("turn_one_up", [[(below1, 0)] + both(w2)], (e,))
    (b,) = step("turn_one_down", [[(above1, 1)] + both(w2)], (a,))
    below2, above2 = up(a, "two"), down(b, "two")
    f = flip(e, 2, "cross")
    new, w3 = update(3, new, (a,))

    def pick(name, ring, flips, after):
        outs = [sum((slots_of((j,), *ring) for j in group), []) for group in flips]
        return step("pick_" + name, outs + [slots_of((0,), *ring)], after)

    (a,) = step("turn_two_up", [[(below2, 1)] + both(w3)], (f,))
    (b,) = step("turn_two_down", [[(above2, 2)] + both(w3)], (a,))
    below3, above3 = up(a, "three"), down(b, "three")
    ring1 = (both(w1), both(above1), [(below2, 0), (above2, 0)], both(below1))
    x, o1, s1 = pick("one", ring1, ((2, 3), (1,)), (a,))
    y1 = flip(x, 2, "chip_one")
    new, again = update(1, new, (s1,))

    (a,) = step("turn_three_up", [[(below3, 1)] + both(e)], (again,))
    (b,) = step("turn_three_down", [[(above3, 2)] + both(e)], (a,))
    below4, above4 = up(a, "four"), down(b, "four")
    ring2 = (both(w2), both(above2, 1), [(below3, 0), (above3, 0)], both(below2, 1))
    x, o1, o2, s2 = step(
        "pick_two",
        [slots_of((2, 3), *ring2), both(o1), slots_of((1,), *ring2), slots_of((0,), *ring2)],
        (a,),
    )
    y2 = flip(x, 2, "chip_two")
    z1, z2 = flip(o1, 1, "core_one"), flip(o2, 1, "core_two")

    (a,) = step("turn_four_up", [[(below4, 1)] + both(f)], (s2, y1, z1, z2))
    (b,) = step("turn_four_down", [[(above4, 2)] + both(f)], (a,))
    below5, above5 = up(a, "five"), down(b, "five")
    ring3 = (both(w3), both(above3, 1), [(below4, 0), (above4, 0)], both(below3, 1))
    x = slots_of((2,), *ring3)
    xa, xb, xc, o3, s3 = step(
        "pick_three",
        [x[:1], x[1:], slots_of((3,), *ring3), slots_of((1,), *ring3), slots_of((0,), *ring3)],
        (a,),
    )
    xa = flip(xa, 2, "chip_three")
    (c,) = step("pass_one", [both(y1, 2)], (s3,))
    t1 = flip(c, 1, "core_pass_one")

    (a,) = step("turn_five_up", [[(below5, 1)]], (t1, y2, xa))
    b, c = step("turn_five_down", [[(above5, 2)], both(y2, 2) + both(o3)], (a,))
    far_low_f, far_high_f = up(a, "last"), down(b, "last")
    z = flip(c, 1, "core_join")
    xb, xc = flip(xb, 2, "chip_three_more"), flip(xc, 3, "both_three")
    places = place(1, (0, 0, 0), (1, 0, 1), (2, 0, 2), (3, 0, 3)) + place(2, (4, 0, 0), (5, 0, 1), (6, 0, 2))
    result = quantize([s1, z1, y1, t1, s2, z2, y2], places, shape, ())

    ring_e = (both(e), both(above4, 1), [(below5, 0), (above5, 0)], both(below4, 1))
    ring_f = (both(f), both(above5, 1), [(far_low_f, 0), (far_high_f, 0)], both(below5, 1))
    pieces = slots_of((1,), *ring_e) + slots_of((1,), *ring_f)
    outs = [[piece] for piece in pieces] + [slots_of((0,), *ring_e), slots_of((0,), *ring_f)]
    *pieces, se, sf = step("pick_last", outs, (result[1], xb))
    pieces = [flip(piece, 1, "core_last") for piece in pieces]
    places = place(3, (0, 0, 0), (1, 2, 1)) + [(2, 0, 2, 0, 3), (3, 0, 2, 1, 3)]
    places += place(0, (4, 0, 0), (5, 0, 2)) + place(2, (1, 0, 3))
    result = quantize([s3, z, xa, xb, se, sf], places, shape, tuple(result))
    places = [(0, 0, 1, 0, 0), (1, 0, 1, 1, 0), (2, 0, 3, 0, 0), (3, 0, 3, 1, 0)]
    result = quantize(pieces, places, shape, tuple(result))
    result = quantize([xc], place(3, (0, 0, 3)), shape, tuple(result))
    return (*new, *result)


def solution(mesh):
    return jax.shard_map(
        body,
        mesh=mesh,
        in_specs=(
            P("ep", "replica", "train"),
            P("ep", "replica", "train"),
            P("ep", "replica", "train"),
            P(),
        ),
        out_specs=(
            P("ep", "replica", "train"),
            P("ep", "replica", "train"),
            P("replica", "ep", None, None, "train"),
            P("replica", "ep", None, None, "train"),
        ),
        check_vma=False,
    )
```

```python
import functools

import jax
import jax.numpy as jnp
from jax import lax
from jax.experimental import pallas as pl
from jax.experimental.pallas import tpu as pltpu
from jax.sharding import PartitionSpec as P

BLOCK = 128
decay_rate = 0.95
step_size = 0.3

ANY = pl.BlockSpec(memory_space=pl.ANY)
SMEM = pl.BlockSpec(memory_space=pltpu.SMEM)
VMEM = pl.BlockSpec(memory_space=pltpu.VMEM)
HBM = pl.BlockSpec(memory_space=pltpu.HBM)
LIMIT = pltpu.CompilerParams(vmem_limit_bytes=8 << 20)


def held(value):
    return pltpu.with_memory_space_constraint(value, pltpu.VMEM)


def outside(value):
    return pltpu.with_memory_space_constraint(value, pltpu.HBM)


def kept(shape, dtype):
    return pltpu.VMEM(shape, dtype)


def cost(bytes_accessed, flops=0):
    return pl.CostEstimate(flops=flops, bytes_accessed=bytes_accessed, transcendentals=0)


def squares_kernel(gradient_ref, out_ref):
    experts, rows, cols = gradient_ref.shape
    step = 64
    total = jnp.zeros((8, cols), jnp.float32)
    for expert in range(experts):

        def add(i, total):
            values = gradient_ref[expert, pl.ds(pl.multiple_of(i * step, step), step), :].astype(jnp.float32)
            return total + jnp.sum((values * values).reshape(step // 8, 8, cols), axis=0)

        total = lax.fori_loop(0, rows // step, add, total)
    tile = sum(total[:, c : c + 128] for c in range(0, cols, 128))
    out_ref[...] = jnp.broadcast_to(jnp.sum(tile, axis=0, keepdims=True), out_ref.shape)


def local_squares(gradient, devices):
    return pl.pallas_call(
        squares_kernel,
        in_specs=[VMEM],
        out_specs=VMEM,
        out_shape=jax.ShapeDtypeStruct((devices, 128), jnp.float32),
        cost_estimate=cost(gradient.size * 2, gradient.size * 2),
        compiler_params=LIMIT,
        name="local_squares",
    )(held(gradient))


def load_kernel(chunk, n, *refs):
    sources, outs, sems = refs[:n], refs[-n - 1 : -1], refs[-1]
    copies = [
        pltpu.make_async_copy(
            source.at[expert, pl.ds(chunk * BLOCK, BLOCK), :], out.at[expert], sems.at[number, expert]
        )
        for number, (source, out) in enumerate(zip(sources, outs))
        for expert in range(out.shape[0])
    ]
    for copy in copies:
        copy.start()
    for copy in copies:
        copy.wait()


def load_rows(values, chunk, after):
    n = len(values)
    shapes = [(value.shape[0], BLOCK, value.shape[2]) for value in values]
    return pl.pallas_call(
        functools.partial(load_kernel, chunk, n),
        in_specs=[HBM] * n + [ANY] * len(after),
        out_specs=[VMEM] * n,
        out_shape=[kept(shape, value.dtype) for shape, value in zip(shapes, values)],
        scratch_shapes=[pltpu.SemaphoreType.DMA((n, shapes[0][0]))],
        cost_estimate=cost(sum(2 * a * b * c * 4 for a, b, c in shapes)),
        compiler_params=LIMIT,
        name="load_rows",
    )(*(outside(value) for value in values), *after)


def new_rows(scale, master, gradient, second):
    clipped = gradient.astype(jnp.float32) * scale
    second_new = decay_rate * second + (1.0 - decay_rate) * clipped * clipped
    return master - step_size * clipped / (jnp.sqrt(second_new) + 1e-08), second_new


def scale_of(count, total_ref):
    square_sum = jnp.sum(jnp.sum(total_ref[...], axis=0, keepdims=True), axis=1, keepdims=True)
    return 1.0 / jnp.sqrt(square_sum / count + 1e-06)


def weights_kernel(count, total_ref, master_ref, gradient_ref, second_ref, weights_out):
    scale = scale_of(count, total_ref)
    step = 32
    for expert in range(master_ref.shape[0]):

        @pl.loop(0, BLOCK // step)
        def _(i):
            here = pl.ds(pl.multiple_of(i * step, step), step)
            master_new, _ = new_rows(
                scale, master_ref[expert, here, :], gradient_ref[expert, here, :], second_ref[expert, here, :]
            )
            weights_out[expert, here, :] = master_new.astype(jnp.bfloat16)


def first_weights(count, total, master, gradient, second):
    return pl.pallas_call(
        functools.partial(weights_kernel, count),
        in_specs=[VMEM] * 4,
        out_specs=VMEM,
        out_shape=kept(master.shape, jnp.bfloat16),
        cost_estimate=cost(master.size * 12, master.size * 20),
        compiler_params=LIMIT,
        name="first_weights",
    )(held(total), held(master), held(gradient), held(second))


def update_kernel(count, chunk, total_ref, *refs):
    sources, (master_out, second_out, weights_out, *scratch) = refs[:3], refs[-10:]
    master_in, gradient_in, second_in, master_new, second_new, in_sems, out_sems = scratch
    scale = scale_of(count, total_ref)
    experts = weights_out.shape[0]
    step, half = 32, BLOCK // 2
    pieces = [(expert, part) for expert in range(experts) for part in range(2)]

    def rows_of(part):
        return pl.ds(part * half, half), pl.ds(chunk * BLOCK + part * half, half)

    arriving, leaving = {}, []
    for expert, part in pieces:
        here, there = rows_of(part)
        arriving[expert, part] = [
            pltpu.make_async_copy(source.at[expert, there, :], place.at[expert, here, :], in_sems.at[n, expert, part])
            for n, (source, place) in enumerate(zip(sources, (master_in, gradient_in, second_in)))
        ]
        for copy in arriving[expert, part]:
            copy.start()
    for expert, part in pieces:
        for copy in arriving[expert, part]:
            copy.wait()

        @pl.loop(0, half // step)
        def _(i):
            here = pl.ds(pl.multiple_of(part * half + i * step, step), step)
            master, second = new_rows(
                scale, master_in[expert, here, :], gradient_in[expert, here, :], second_in[expert, here, :]
            )
            master_new[expert, here, :] = master
            second_new[expert, here, :] = second
            weights_out[expert, here, :] = master.astype(jnp.bfloat16)

        here, there = rows_of(part)
        for n, (place, out) in enumerate(((master_new, master_out), (second_new, second_out))):
            copy = pltpu.make_async_copy(
                place.at[expert, here, :], out.at[expert, there, :], out_sems.at[n, expert, part]
            )
            copy.start()
            leaving.append(copy)
    for copy in leaving:
        copy.wait()


def update_rows(count, total, master, gradient, second, chunk, earlier, after):
    experts, rows, cols = master.shape
    shape = (experts, BLOCK, cols)
    size = experts * BLOCK * cols
    return pl.pallas_call(
        functools.partial(update_kernel, count, chunk),
        in_specs=[VMEM] + [HBM] * 3 + [ANY] * (len(earlier) + len(after)),
        out_specs=[HBM, HBM, VMEM],
        out_shape=[
            jax.ShapeDtypeStruct(master.shape, jnp.float32),
            jax.ShapeDtypeStruct(master.shape, jnp.float32),
            kept(shape, jnp.bfloat16),
        ],
        input_output_aliases={4: 0, 5: 1} if earlier else {},
        scratch_shapes=[
            pltpu.VMEM(shape, jnp.float32),
            pltpu.VMEM(shape, jnp.bfloat16),
            pltpu.VMEM(shape, jnp.float32),
            pltpu.VMEM(shape, jnp.float32),
            pltpu.VMEM(shape, jnp.float32),
            pltpu.SemaphoreType.DMA((3, experts, 2)),
            pltpu.SemaphoreType.DMA((2, experts, 2)),
        ],
        cost_estimate=cost(size * 20, size * 20),
        compiler_params=LIMIT,
        name="update_rows",
    )(held(total), outside(master), outside(gradient), outside(second), *earlier, *after)


def slot_table(placement, holders, per_device):
    matches = (placement[:, None, :] == jnp.arange(holders, dtype=jnp.int32)[None, :, None]).astype(jnp.int32)
    rank_within = jnp.cumsum(matches, axis=-1) - 1
    expert_ids = jnp.arange(placement.shape[-1], dtype=jnp.int32)
    slot_numbers = jnp.arange(per_device, dtype=jnp.int32)
    selected = matches[..., None, :] * (rank_within[..., None, :] == slot_numbers[:, None]).astype(jnp.int32)
    return jnp.sum(selected * expert_ids, axis=-1)


def step_kernel(moves, n, *refs):
    table_ref = refs[n]
    arrays, outs = refs[:n], refs[len(refs) - 1 - max(m[0] for m in moves) :]
    for out, place, entry, sources in moves:
        if entry is None:
            array, index = sources
            outs[out][place] = arrays[array][index]
            continue
        code = table_ref[entry]
        for steps, (low, high) in enumerate(sources):
            if low[0] == high[0]:

                @pl.when(code // 2 == steps)
                def _():
                    outs[out][place] = arrays[low[0]][low[1] + code % 2]

            else:
                for number, (array, index) in enumerate((low, high)):

                    @pl.when(code == 2 * steps + number)
                    def _():
                        outs[out][place] = arrays[array][index]


def make_step(table, outs, after=(), work=0):
    arrays, moves = [], []

    def number_of(array):
        for number, known in enumerate(arrays):
            if known is array:
                return number
        arrays.append(array)
        return len(arrays) - 1

    for out, pieces in enumerate(outs):
        for place, (first, second) in enumerate(pieces):
            if isinstance(first, int):
                sources = [tuple((number_of(a), i) for a, i in pair) for pair in second]
                moves.append((out, place, first, sources))
            else:
                moves.append((out, place, None, (number_of(first), second)))
    rows, cols = arrays[0].shape[1:]
    tables = [table] if any(move[2] is not None for move in moves) else []
    return pl.pallas_call(
        functools.partial(step_kernel, moves, len(arrays)),
        in_specs=[VMEM] * len(arrays) + [SMEM] * len(tables) + [ANY] * len(after),
        out_specs=[VMEM] * len(outs),
        out_shape=[kept((len(pieces), rows, cols), jnp.bfloat16) for pieces in outs],
        cost_estimate=cost(max(int(work * 3.3e6), len(moves) * rows * cols * 4)),
        compiler_params=LIMIT,
        name="make_step",
    )(*(held(a) for a in arrays), *tables, *after)


def quantize_kernel(places, *refs):
    n = len({place[0] for place in places})
    replica = lax.axis_index("replica")
    parts, earlier, (out_ref, scales_ref, ready, sems) = refs[:n], refs[n:-4], refs[-4:]
    scales_ref[...] = earlier[1][...] if earlier else jnp.zeros_like(scales_ref)
    rows, cols = parts[0].shape[1:]
    blocks = cols // BLOCK
    copies = []
    for number, (part, index, flip, slot, chunk) in enumerate(places):
        block_row = jnp.bitwise_xor(replica, flip) * 4 + chunk
        tops = []
        for block in range(blocks):
            values = jnp.abs(parts[part][index, :, block * BLOCK : (block + 1) * BLOCK].astype(jnp.float32))
            tops.append(jnp.max(values.reshape(rows // 8, 8, BLOCK), axis=0).max(axis=0, keepdims=True))
        tops = jnp.concatenate(tops + [jnp.zeros((8 - blocks, BLOCK), jnp.float32)], axis=0)
        largest = jnp.max(tops, axis=1, keepdims=True) + 1e-06
        inverse = 1.0 / largest
        for block in range(blocks):
            at = slice(block * BLOCK, (block + 1) * BLOCK)
            values = parts[part][index, :, at].astype(jnp.float32)
            ready[number, :, at] = (values * inverse[block : block + 1, :]).astype(jnp.bfloat16)
        lane = lax.broadcasted_iota(jnp.int32, (1, blocks), 1)
        line = jnp.zeros((1, blocks), jnp.float32)
        for block in range(blocks):
            line = jnp.where(lane == block, largest[block : block + 1, :], line)
        scales_ref[0, 0, slot, pl.ds(block_row, 1), :] = line
        target = out_ref.at[0, 0, slot, pl.ds(pl.multiple_of(block_row * BLOCK, BLOCK), BLOCK), :]
        copies.append(pltpu.make_async_copy(ready.at[number], target, sems.at[number]))
        copies[-1].start()
    for copy in copies:
        copy.wait()


def quantize(parts, places, shape, earlier):
    rows, cols = parts[0].shape[1:]
    scales_shape = (1, 1, shape[2], shape[3] // BLOCK, cols // BLOCK)
    n = len(parts)
    return pl.pallas_call(
        functools.partial(quantize_kernel, tuple(places)),
        in_specs=[VMEM] * n + ([ANY, VMEM] if earlier else []),
        out_specs=[HBM, VMEM],
        out_shape=[jax.ShapeDtypeStruct(shape, jnp.bfloat16), jax.ShapeDtypeStruct(scales_shape, jnp.float32)],
        input_output_aliases={n: 0} if earlier else {},
        scratch_shapes=[
            pltpu.VMEM((len(places), rows, cols), jnp.bfloat16),
            pltpu.SemaphoreType.DMA((len(places),)),
        ],
        cost_estimate=cost(len(places) * rows * cols * 4, len(places) * rows * cols * 5),
        compiler_params=pltpu.CompilerParams(vmem_limit_bytes=12 << 20),
        name="quantize_rows",
    )(*(held(p) for p in parts), *earlier)


def body(master, gradient, second, placement):
    n_train, n_replica, n_ep = (lax.axis_size(a) for a in ("train", "replica", "ep"))
    experts, rows, cols = master.shape
    count = float(master.size * n_train * n_replica * n_ep)
    replica, holder = lax.axis_index("replica"), lax.axis_index("ep")

    slots = slot_table(placement, n_ep, experts)[:, holder]
    order = jnp.bitwise_xor(replica, jnp.arange(n_replica, dtype=jnp.int32))
    named = slots[order].reshape(-1)
    table = 2 * ((named // 2 - holder) % n_ep) + named % 2

    devices = ("train", "replica", "ep")
    part = local_squares(gradient, n_train * n_replica * n_ep)
    master1, gradient1, second1 = load_rows((master, gradient, second), 1, (part, table))
    total = lax.all_to_all(part, devices, 0, 0, tiled=True)

    def send(value, axis, order, name):
        with jax.named_scope(name):
            return lax.ppermute(value, axis, order)

    def up(value, name):
        return send(value, "ep", [(i, (i + 1) % n_ep) for i in range(n_ep)], name + "_up")

    def down(value, name):
        return send(value, "ep", [(i, (i - 1) % n_ep) for i in range(n_ep)], name + "_down")

    def flip(value, by, name):
        return send(value, "replica", [(i, i ^ by) for i in range(n_replica)], name)

    def step(name, outs, after=()):
        with jax.named_scope(name):
            return make_step(table, outs, tuple(after))

    def both(array, first=0):
        return [(array, first), (array, first + 1)]

    def slots_of(flips, here, above, far, below):
        return [(2 * j + k, [here, above, far, below]) for j in flips for k in range(2)]

    def update(chunk, earlier, after=()):
        *new, weights = update_rows(count, total, master, gradient, second, chunk, tuple(earlier), after)
        return new, weights

    def place(chunk, *entries):
        return [(part, index + k, j, k, chunk) for part, index, j in entries for k in range(2)]

    shape = (1, 1, experts, n_replica * rows, cols)

    w1 = first_weights(count, total, master1, gradient1, second1)
    below1, above1 = up(w1, "one"), down(w1, "one")
    new, e = update(0, (), (w1,))
    new, w2 = update(2, new)

    (a,) = step("turn_one_up", [[(below1, 0)]], (e,))
    (b,) = step("turn_one_down", [[(above1, 1)]], (a,))
    far_low1, far_high1 = up(a, "on"), down(b, "on")
    p, q = step("next_two", [[(w2, 0)], [(w2, 1)]], (b,))
    below20, above20 = up(p, "two_low"), down(p, "two_low")
    below21, above21 = up(q, "two_high"), down(q, "two_high")
    above2, below2 = [(above20, 0), (above21, 0)], [(below20, 0), (below21, 0)]
    f = flip(e, 2, "cross")
    new, w3 = update(3, new, (a,))

    def pick(name, ring, flips, after):
        outs = [sum((slots_of((j,), *ring) for j in group), []) for group in flips]
        return step("pick_" + name, outs + [slots_of((0,), *ring)], after)

    ring1 = (both(w1), both(above1), [(far_low1, 0), (far_high1, 0)], both(below1))
    x, o1, s1 = pick("one", ring1, ((2, 3), (1,)), (q,))
    y1 = flip(x, 2, "chip_one")
    (a,) = step("turn_two_up", [[below2[0]] + both(w3)], (f, s1))
    (b,) = step("turn_two_down", [[above2[1]] + both(w3)], (a,))
    below3, above3 = up(a, "three"), down(b, "three")
    new, again = update(1, new, (s1,))

    (a,) = step("turn_three_up", [[(below3, 1)] + both(e)], (again,))
    (b,) = step("turn_three_down", [[(above3, 2)] + both(e)], (a,))
    below4, above4 = up(a, "four"), down(b, "four")
    ring2 = (both(w2), above2, [(below3, 0), (above3, 0)], below2)
    x, o1, o2, s2 = step(
        "pick_two",
        [slots_of((2, 3), *ring2), both(o1), slots_of((1,), *ring2), slots_of((0,), *ring2)],
        (a,),
    )
    y2 = flip(x, 2, "chip_two")
    z1 = flip(o1, 1, "core_one")

    (a,) = step("turn_four_up", [[(below4, 1)] + both(f)], (s2, y1, z1))
    (b,) = step("turn_four_down", [[(above4, 2)] + both(f)], (a,))
    below5, above5 = up(a, "five"), down(b, "five")
    ring3 = (both(w3), both(above3, 1), [(below4, 0), (above4, 0)], both(below3, 1))
    x = slots_of((2,), *ring3)
    xa, xb, xc, o3, s3 = step(
        "pick_three",
        [x[:1], x[1:], slots_of((3,), *ring3), slots_of((1,), *ring3), slots_of((0,), *ring3)],
        (a,),
    )
    xa = flip(xa, 2, "chip_three")
    (c,) = step("pass_one", [both(y1, 2)], (s3,))
    t1 = flip(c, 1, "core_pass_one")

    (a,) = step("turn_five_up", [[(below5, 1)]], (t1, y2, xa))
    b, c = step("turn_five_down", [[(above5, 2)], both(y2, 2) + both(o3) + both(o2)], (a,))
    far_low_f, far_high_f = up(a, "last"), down(b, "last")
    z = flip(c, 1, "core_join")
    xb, xc = flip(xb, 2, "chip_three_more"), flip(xc, 3, "both_three")
    places = place(1, (0, 0, 0), (1, 0, 1), (2, 0, 2), (3, 0, 3)) + place(2, (4, 0, 0), (5, 0, 2))
    result = quantize([s1, z1, y1, t1, s2, y2], places, shape, ())

    ring_e = (both(e), both(above4, 1), [(below5, 0), (above5, 0)], both(below4, 1))
    ring_f = (both(f), both(above5, 1), [(far_low_f, 0), (far_high_f, 0)], both(below5, 1))
    pieces = slots_of((1,), *ring_e) + slots_of((1,), *ring_f)
    outs = [[piece] for piece in pieces] + [slots_of((0,), *ring_e), slots_of((0,), *ring_f)]
    *pieces, se, sf = step("pick_last", outs, (result[1], xb))
    pieces = [flip(piece, 1, "core_last") for piece in pieces]
    places = place(3, (0, 0, 0), (1, 2, 1)) + [(2, 0, 2, 0, 3), (3, 0, 2, 1, 3)]
    places += place(0, (4, 0, 0), (5, 0, 2)) + place(2, (1, 4, 1), (1, 0, 3))
    result = quantize([s3, z, xa, xb, se, sf], places, shape, tuple(result))
    places = [(0, 0, 1, 0, 0), (1, 0, 1, 1, 0), (2, 0, 3, 0, 0), (3, 0, 3, 1, 0)]
    result = quantize(pieces, places, shape, tuple(result))
    result = quantize([xc], place(3, (0, 0, 3)), shape, tuple(result))
    return (*new, *result)


def solution(mesh):
    return jax.shard_map(
        body,
        mesh=mesh,
        in_specs=(
            P("ep", "replica", "train"),
            P("ep", "replica", "train"),
            P("ep", "replica", "train"),
            P(),
        ),
        out_specs=(
            P("ep", "replica", "train"),
            P("ep", "replica", "train"),
            P("replica", "ep", None, None, "train"),
            P("replica", "ep", None, None, "train"),
        ),
        check_vma=False,
    )
```
